128 devices in a mesh: pair: 64 (over x, z_hi, y, core), ga: 2 (over z_lo).
Axes of the slice: x: 4, y: 4, z: 4 (z_hi: 2, z_lo: 2; z = z_hi * 2 + z_lo), core: 2. Of those that a mesh axis runs over, the one named last changes fastest.
Arguments:
- pair_valence: bfloat16 [64, 16384], P(None, 'ga'), may hold values from -6 to 6
- screened: bfloat16 [16384, 16384], P('ga', 'pair'), may hold values from -0.046875 to 0.046875
- pair_conduction: bfloat16 [65536, 16384], P(('pair', 'ga')), may hold values from -0.4375 to 0.4375
- pair_mixed: bfloat16 [8192, 16384], P('ga', 'pair'), may hold values from -3.5 to 3.5
- coulomb: float32 [16384], P('pair'), may hold values from 0.2 to 5
Outputs:
- direct: float32 [65536, 64], P(('pair', 'ga'))
- exchange: float32 [8192, 512], P(('ga', 'pair'))
The draws below stay inside these ranges and needn't reach their ends.
All inputs are finite; a program needn't handle non-finite values.
Results may differ from the reference program's by a relative error of at most 0.0029.
Values may be sent and summed in bfloat16 or wider, within the bound.
A program may use at most 192 MiB of HBM per device.

```python
import math
import jax
import jax.numpy as jnp

NC = 256
NG = 16384
V_WIN = 2
VV = 64
NCC = 65536
NVC = 8192


def spiked(result, own_key, source, target, blocks, factor):
    owner, partner = [(jnp.arange(result.shape[position]) // (result.shape[position] // blocks)).reshape([-1 if axis == position else 1 for axis in range(result.ndim)]) for position in (source, target)]
    chosen = jax.random.permutation(own_key, blocks)[partner]
    strong = (owner == chosen) | (owner == (partner + blocks // 2) % blocks)
    return jnp.where(strong, factor * result, result)


def shard_levels(key, extent, pieces, low, top_value):
    def one(position, parts):
        steps = jax.random.uniform(jax.random.fold_in(jax.random.fold_in(key, 6), position), (parts,), jnp.float32, low / len(pieces), top_value / len(pieces))
        return jnp.repeat(jnp.exp(steps), extent[position] // parts).reshape((-1,) + (1,) * (len(extent) - position - 1))

    gain = one(*pieces[0])
    for cut in pieces[1:]:
        gain = gain * one(*cut)
    return gain


def noise(stream_key, extent, deviation, bound, split=(), kind=jnp.bfloat16):
    drawn = jax.random.normal(stream_key, extent, jnp.float32) * deviation
    if len(split) > 0:
        drawn = shard_levels(stream_key, extent, split, -0.22, 0.18) * drawn
    return jnp.clip(drawn, min=-bound, max=bound).astype(kind)


def heavy_noise(stream_key, dims, width, reach, cuts, heavy, held_as=jnp.bfloat16):
    drawn = width * jax.random.normal(stream_key, dims, jnp.float32)
    if cuts:
        drawn = drawn * shard_levels(stream_key, dims, cuts, -0.22, 0.18)
    return jnp.clip(spiked(drawn, jax.random.fold_in(stream_key, 3), *heavy), -reach, reach).astype(held_as)


def setup_inputs(seed: int = 0) -> dict:
    key_of = jax.random.split(jax.random.key(seed), 6)
    pair_valence = noise(key_of[0], (VV, NG), 1.0, 6.0, ((1, 2),))
    screened = noise(key_of[1], (NG, NG), NG ** -0.5, 0.046875, ((0, 2), (1, 64)))
    pair_conduction = heavy_noise(key_of[2], (NCC, NG), (NG ** -0.5), 0.4375, ((0, 128),), (1, 0, 128, 5.5))
    pair_mixed = heavy_noise(key_of[3], (NVC, NG), (NG ** -0.25), 3.5, ((0, 2), (1, 64)), (1, 0, 64, 4.0))
    coulomb = jnp.clip(jnp.exp(math.log(5.0) - 3.218876 * jax.random.uniform(key_of[4], (NG,), jnp.float32) ** shard_levels(key_of[4], (NG,), ((0, 64),), -0.2, 0.2)), 0.2, 5.0)
    return {"pair_valence": pair_valence, "screened": screened, "pair_conduction": pair_conduction, "pair_mixed": pair_mixed, "coulomb": coulomb}


def reference(pair_valence, screened, pair_conduction, pair_mixed, coulomb):
    images = jnp.dot(pair_valence, screened, preferred_element_type=jnp.float32).astype(jnp.bfloat16)
    direct = jnp.dot(pair_conduction, images.T, preferred_element_type=jnp.float32)
    window = pair_mixed[:V_WIN * NC]
    scaled = (window.astype(jnp.float32) * coulomb).astype(jnp.bfloat16)
    exchange = jnp.dot(pair_mixed, scaled.T, preferred_element_type=jnp.float32)
    return direct, exchange
```

```python
import jax
import jax.numpy as jnp
from jax import lax
from jax.sharding import PartitionSpec as P

NC = 256
V_WIN = 2


def spread(value, axis, source):
    kept = jnp.where(lax.axis_index(axis) == source, value, 0).astype(value.dtype)
    return lax.psum(kept, axis)


def local(pair_valence, screened, pair_conduction, pair_mixed, coulomb):
    slab = jnp.dot(pair_valence, screened, preferred_element_type=jnp.float32)
    images = lax.psum(slab, "ga").astype(jnp.bfloat16)
    images = lax.all_gather(images, "pair", axis=1, tiled=True)
    direct = jnp.einsum("ck,vk->cv", pair_conduction, images, preferred_element_type=jnp.float32)
    window_count = V_WIN * NC
    window_top = pair_mixed[:window_count]
    window = spread(window_top, "ga", 0)
    scaled = (window.astype(jnp.float32) * coulomb).astype(jnp.bfloat16)
    picked = pair_mixed
    exchange = lax.psum_scatter(
        jnp.einsum("gk,xk->gx", picked, scaled, preferred_element_type=jnp.float32),
        "pair",
        scatter_dimension=0,
        tiled=True,
    )
    return (direct, exchange)


def solution(mesh):
    return jax.shard_map(
        local,
        mesh=mesh,
        in_specs=(
            P(None, "ga"),
            P("ga", "pair"),
            P(("pair", "ga"), None),
            P("ga", "pair"),
            P("pair"),
        ),
        out_specs=(P(("pair", "ga"), None), P(("ga", "pair"), None)),
        check_vma=False,
    )
```

```python
import jax
import jax.numpy as jnp
from jax import lax
from jax.experimental import pallas as pl
from jax.experimental.pallas import tpu as pltpu
from jax.sharding import PartitionSpec as P

MESH = pl.DeviceIdType.MESH
BF = jnp.bfloat16
F32 = jnp.float32
KB = 256
MESSAGES = 96


def dot_t(a, b):
    return lax.dot_general(a, b, (((1,), (1,)), ((), ())), preferred_element_type=F32)


def kernel(
    pv_hbm,
    w_hbm,
    pc_hbm,
    pm_hbm,
    cl_hbm,
    direct_ref,
    exchange_ref,
    pv_buf,
    w_buf,
    pc_buf,
    a_buf,
    b_buf,
    win_buf,
    cl_buf,
    part_buf,
    part_recv,
    img,
    snd1,
    opp_recv,
    dir_recv,
    comb_recv,
    acc1,
    snd2,
    recv2,
    acc2,
    snd3,
    recv3,
    load_sem,
    ss,
    rs,
):
    pair = lax.axis_index("pair")
    ga = lax.axis_index("ga")
    c = pair % 2
    y = (pair // 2) % 4
    zh = (pair // 8) % 2
    x = pair // 16
    z = zh * 2 + ga

    def dev(dx=0, dy=0, dz=0, dc=0):
        xx, yy, zz, cc = (x + dx) % 4, (y + dy) % 4, (z + dz) % 4, (c + dc) % 2
        return {"pair": ((xx * 2 + zz // 2) * 4 + yy) * 2 + cc, "ga": zz % 2}

    core_peer = dev(dc=1)
    ga_peer = {"pair": pair, "ga": 1 - ga}
    z_half = dev(dz=2)
    peers = [core_peer] + [dev(**{d: o}) for d in ("dx", "dy", "dz") for o in (1, 2, 3)]

    count = [0]
    sent = []

    def message(src, dst, device):
        i = count[0]
        count[0] += 1
        copy = pltpu.make_async_remote_copy(
            src_ref=src,
            dst_ref=dst,
            send_sem=ss.at[i],
            recv_sem=rs.at[i],
            device_id=device,
            device_id_type=MESH,
        )
        return copy

    def send(copy):
        copy.start()
        sent.append(copy)

    loads = [0]

    def load(src, dst):
        i = loads[0]
        loads[0] += 1
        return pltpu.make_async_copy(src, dst, load_sem.at[i])

    barrier = pltpu.get_barrier_semaphore()
    for peer in peers:
        pl.semaphore_signal(barrier, inc=1, device_id=peer, device_id_type=MESH)

    ld_win = load(pm_hbm.at[0, 0], win_buf)
    ld_cl = load(cl_hbm, cl_buf)
    ld_pv = load(pv_hbm, pv_buf)
    ld_w = [load(w_hbm.at[pl.ds(k * 2048, 2048)], w_buf.at[pl.ds(k * 2048, 2048)]) for k in range(4)]
    ld_a = load(pm_hbm.at[:, :, :, c], a_buf.at[c])
    ld_pc = [load(pc_hbm.at[pl.ds(k * 128, 128)], pc_buf.at[pl.ds(k * 128, 128)]) for k in range(4)]

    @pl.when(ga == 0)
    def _():
        ld_win.start()

    ld_cl.start()
    ld_pv.start()
    for copy in ld_w:
        copy.start()
    ld_a.start()

    pl.semaphore_wait(barrier, len(peers))

    m_a = message(pm_hbm.at[:, :, :, 1 - c], a_buf.at[c], core_peer)
    send(m_a)

    m_b_ga = [message(b_buf.at[c, n], b_buf.at[c, n], ga_peer) for n in range(2)]
    m_b_core = [message(b_buf.at[c, n], b_buf.at[c, n], core_peer) for n in range(2)]

    @pl.when(ga == 0)
    def _():
        ld_win.wait()

    ld_cl.wait()

    @pl.when(ga == 0)
    def _():
        v = cl_buf[...]
        for n in range(2):
            rows = win_buf[2 * n : 2 * n + 2].reshape(256, KB)
            b_buf[c, n] = (rows.astype(F32) * v).astype(BF)
            m_b_ga[n].start()
            m_b_core[n].start()

    ld_pv.wait()
    part = None
    for k in range(4):
        ld_w[k].wait()
        term = jnp.dot(
            pv_buf[:, k * 2048 : (k + 1) * 2048],
            w_buf[k * 2048 : (k + 1) * 2048, :],
            preferred_element_type=F32,
        )
        part = term if part is None else part + term
    part_buf[...] = part.reshape(2, 32, KB)
    m_part = message(part_buf.at[1 - ga], part_recv, ga_peer)
    send(m_part)
    for copy in ld_pc:
        copy.start()

    ld_a.wait()

    def tile_rows(s, r, d, h):
        rows = pl.ds(r * 32, 32)
        if r == 0:
            value = a_buf[s, (x + d) % 4, h, :, rows, :]
        else:
            value = a_buf[s, :, h, (y + d) % 4, rows, :]
        return value.reshape(128, KB)

    def tile(r, n, d, halves):
        total = None
        for s in range(2):
            rows = [tile_rows(s, r, d, h) for h in halves]
            rows = rows[0] if len(rows) == 1 else jnp.concatenate(rows, axis=0)
            term = dot_t(rows, b_buf[s, n])
            total = term if total is None else total + term
        return total.reshape(len(halves), 4, 32, 256)

    def first(r, d):
        return dev(dx=d) if r == 0 else dev(dy=d)

    def second(r, d):
        return dev(dy=d) if r == 0 else dev(dx=d)

    streams = [(r, n) for n in range(2) for r in range(2)]
    m_opp, m_dir, m_comb, m_two, m_three = {}, {}, {}, {}, {}
    for r, n in streams:
        for way, d in ((0, 1), (1, 3)):
            m_opp[r, n, way] = message(snd1.at[r, n, 0, way], opp_recv.at[r, n, way], first(r, d))
            m_dir[r, n, way] = message(snd1.at[r, n, 1, way], dir_recv.at[r, n, way], first(r, d))
            m_comb[r, n, way] = message(snd1.at[r, n, 2, way], comb_recv.at[r, n, way], first(r, d))
        for e in (1, 2, 3):
            m_two[r, n, e] = message(snd2.at[r, n, e - 1], recv2.at[r, n, e - 1], second(r, e))
        m_three[r, n] = message(snd3.at[r, n], recv3.at[r, n], z_half)

    def rs_open(n):
        for r in range(2):
            snd1[r, n, 0] = tile(r, n, 2, (0, 1)).astype(BF)
            m_opp[r, n, 0].start()
            m_opp[r, n, 1].start()
        for r in range(2):
            snd1[r, n, 1, 0] = tile(r, n, 1, (1,))[0].astype(BF)
            m_dir[r, n, 0].start()
            snd1[r, n, 1, 1] = tile(r, n, 3, (0,))[0].astype(BF)
            m_dir[r, n, 1].start()

    def rs_comb(n):
        for r in range(2):
            for way, d, h in ((0, 1, 0), (1, 3, 1)):
                own = tile(r, n, d, (h,))[0]
                m_opp[r, n, way].wait_recv()
                snd1[r, n, 2, way] = (own + opp_recv[r, n, way].astype(F32)).astype(BF)
                m_comb[r, n, way].start()
        for r in range(2):
            acc1[r, n] = tile(r, n, 0, (0, 1))

    def rs_second(n):
        for r in range(2):
            for way in range(2):
                m_dir[r, n, way].wait_recv()
            for way in range(2):
                m_comb[r, n, way].wait_recv()
            for h in range(2):
                acc1[r, n, h] = acc1[r, n, h] + dir_recv[r, n, 1 - h].astype(F32) + comb_recv[r, n, h].astype(F32)
            me = y if r == 0 else x
            for e in (2, 1, 3):
                snd2[r, n, e - 1] = acc1[r, n, :, (me + e) % 4].astype(BF)
                m_two[r, n, e].start()

    def rs_third(n):
        for r in range(2):
            me = y if r == 0 else x
            for e in (1, 3, 2):
                m_two[r, n, e].wait_recv()
            total = acc1[r, n, :, me]
            for e in (1, 3, 2):
                total = total + recv2[r, n, e - 1].astype(F32)
            acc2[r, n] = total
            snd3[r, n] = acc2[r, n, 1 - zh].astype(BF)
            m_three[r, n].start()

    def rs_last(n):
        for r in range(2):
            m_three[r, n].wait_recv()
            exchange_ref[r * 32 : r * 32 + 32, n * 256 : n * 256 + 256] = acc2[r, n, zh] + recv3[r, n].astype(F32)

    m_z = [message(img.at[c, zh, x, y, ga], img.at[c, zh, x, y, ga], dev(dz=f)) for f in (1, 2, 3)]

    def gather_axis(h, d):
        return dev(dx=d) if h == 0 else dev(dy=d)

    def gather_second(h, d):
        return dev(dy=d) if h == 0 else dev(dx=d)

    def line(cc, h, e):
        return img.at[cc, h, :, (y + e) % 4] if h == 0 else img.at[cc, h, (x + e) % 4]

    def half_line(cc, h, e, part):
        some = pl.ds(2 * part, 2)
        return img.at[cc, h, some, (y + e) % 4] if h == 0 else img.at[cc, h, (x + e) % 4, some]

    m_g1, m_g2, m_relay, m_fwd = {}, {}, {}, {}
    for h in range(2):
        mine = img.at[c, h, x, y]
        for d in (1, 2, 3):
            m_g1[h, d] = message(mine, mine, gather_axis(h, d))
        for d in (1, 3):
            m_g2[h, d] = message(line(c, h, 0), line(c, h, 0), gather_second(h, d))
        m_relay[h, 1] = message(half_line(c, h, 3, 0), half_line(c, h, 3, 0), gather_second(h, 1))
        m_relay[h, 3] = message(half_line(c, h, 1, 1), half_line(c, h, 1, 1), gather_second(h, 3))
        for e in range(4):
            m_fwd[h, e] = message(line(c, h, e), line(c, h, e), core_peer)

    def direct_group(cc, h, e, begin=False):
        total = None
        for j in range(4):
            xx, yy = (j, (y + e) % 4) if h == 0 else ((x + e) % 4, j)
            block = ((xx * 2 + h) * 4 + yy) * 2 + cc
            cols = pl.ds(pl.multiple_of(block * KB, KB), KB)
            term = dot_t(pc_buf[:, cols], img[cc, h, xx, yy].reshape(64, KB))
            total = term if total is None else total + term
        direct_ref[...] = total if begin else direct_ref[...] + total

    m_a.wait_recv()

    @pl.when(ga == 0)
    def _():
        m_b_core[0].wait_recv()
        rs_open(0)

    m_part.wait_recv()
    img[c, zh, x, y, ga] = (part_buf[ga] + part_recv[...]).astype(BF)
    for copy in m_z:
        send(copy)

    @pl.when(ga == 1)
    def _():
        m_b_ga[0].wait_recv()
        m_b_core[0].start()

    for copy in m_z:
        copy.wait_recv()
    for h in range(2):
        for d in (2, 1, 3):
            send(m_g1[h, d])

    @pl.when(ga == 1)
    def _():
        m_b_core[0].wait_recv()
        rs_open(0)

    for h in range(2):
        for d in (1, 3, 2):
            m_g1[h, d].wait_recv()
        for d in (1, 3):
            send(m_g2[h, d])
    for h in range(2):
        send(m_fwd[h, 0])

    rs_comb(0)

    @pl.when(ga == 1)
    def _():
        m_b_ga[1].wait_recv()
        m_b_core[1].start()

    m_b_core[1].wait_recv()
    rs_open(1)

    for h in range(2):
        for d in (1, 3):
            m_g2[h, d].wait_recv()
            send(m_relay[h, d])
    for h in range(2):
        for e in (1, 3):
            send(m_fwd[h, e])

    rs_second(0)
    rs_comb(1)

    for copy in ld_pc:
        copy.wait()
    for h in range(2):
        direct_group(c, h, 0, begin=h == 0)
    for h in range(2):
        m_fwd[h, 0].wait_recv()
        direct_group(1 - c, h, 0)

    rs_third(0)

    for h in range(2):
        for d in (1, 3):
            m_relay[h, d].wait_recv()
        send(m_fwd[h, 2])
    for h in range(2):
        for e in (1, 3):
            direct_group(c, h, e)

    rs_second(1)

    for h in range(2):
        for e in (1, 3):
            m_fwd[h, e].wait_recv()
            direct_group(1 - c, h, e)

    rs_last(0)
    rs_third(1)

    for h in range(2):
        direct_group(c, h, 2)
        m_fwd[h, 2].wait_recv()
        direct_group(1 - c, h, 2)

    rs_last(1)

    for copy in sent:
        copy.wait_send()

    @pl.when(ga == 0)
    def _():
        for n in range(2):
            m_b_ga[n].wait_send()

    for n in range(2):
        m_b_core[n].wait_send()
    for group in (m_opp, m_dir, m_comb, m_two, m_three):
        for copy in group.values():
            copy.wait_send()


def solution(mesh):
    def local(pair_valence, screened, pair_conduction, pair_mixed, coulomb):
        anywhere = pl.BlockSpec(memory_space=pl.ANY)
        vmem = pl.BlockSpec(memory_space=pltpu.VMEM)
        return pl.pallas_call(
            kernel,
            out_shape=(
                jax.ShapeDtypeStruct((512, 64), F32),
                jax.ShapeDtypeStruct((64, 512), F32),
            ),
            in_specs=[anywhere] * 5,
            out_specs=(vmem, vmem),
            scratch_shapes=[
                pltpu.VMEM((64, 8192), BF),
                pltpu.VMEM((8192, KB), BF),
                pltpu.VMEM((512, 16384), BF),
                pltpu.VMEM((2, 4, 2, 4, 64, KB), BF),
                pltpu.VMEM((2, 2, 256, KB), BF),
                pltpu.VMEM((4, 2, 64, KB), BF),
                pltpu.VMEM((1, KB), F32),
                pltpu.VMEM((2, 32, KB), F32),
                pltpu.VMEM((32, KB), F32),
                pltpu.VMEM((2, 2, 4, 4, 2, 32, KB), BF),
                pltpu.VMEM((2, 2, 3, 2, 4, 32, 256), BF),
                pltpu.VMEM((2, 2, 2, 4, 32, 256), BF),
                pltpu.VMEM((2, 2, 2, 4, 32, 256), BF),
                pltpu.VMEM((2, 2, 2, 4, 32, 256), BF),
                pltpu.VMEM((2, 2, 2, 4, 32, 256), F32),
                pltpu.VMEM((2, 2, 3, 2, 32, 256), BF),
                pltpu.VMEM((2, 2, 3, 2, 32, 256), BF),
                pltpu.VMEM((2, 2, 2, 32, 256), F32),
                pltpu.VMEM((2, 2, 32, 256), BF),
                pltpu.VMEM((2, 2, 32, 256), BF),
                pltpu.SemaphoreType.DMA((16,)),
                pltpu.SemaphoreType.DMA((MESSAGES,)),
                pltpu.SemaphoreType.DMA((MESSAGES,)),
            ],
            compiler_params=pltpu.CompilerParams(
                collective_id=0, has_side_effects=True, vmem_limit_bytes=60 << 20
            ),
            cost_estimate=pl.CostEstimate(flops=3 << 30, bytes_accessed=24 << 20, transcendentals=0),
        )(
            pair_valence,
            screened,
            pair_conduction,
            pair_mixed.reshape(4, 2, 4, 2, 64, KB),
            coulomb.reshape(1, KB),
        )

    return jax.shard_map(
        local,
        mesh=mesh,
        in_specs=(
            P(None, "ga"),
            P("ga", "pair"),
            P(("pair", "ga"), None),
            P("ga", "pair"),
            P("pair"),
        ),
        out_specs=(P(("pair", "ga"), None), P(("ga", "pair"), None)),
        check_vma=False,
    )
```

```python
import jax
import jax.numpy as jnp
from jax import lax
from jax.experimental import pallas as pl
from jax.experimental.pallas import tpu as pltpu
from jax.sharding import PartitionSpec as P

MESH = pl.DeviceIdType.MESH
BF = jnp.bfloat16
F32 = jnp.float32
KB = 256
CHUNKS = 4
W = 512 // CHUNKS


def dot_t(a, b):
    return lax.dot_general(a, b, (((1,), (1,)), ((), ())), preferred_element_type=F32)


def kernel(
    pv_hbm,
    w_hbm,
    pc_hbm,
    pm_hbm,
    cl_hbm,
    direct_ref,
    exchange_ref,
    pv_buf,
    w_buf,
    pc_buf,
    a_buf,
    b_buf,
    win_buf,
    cl_buf,
    part_buf,
    part_recv,
    img,
    snd1,
    opp_recv,
    near_recv,
    acc1,
    snd2,
    recv2,
    dacc,
    load_sem,
    send_sem,
    b_sem,
    rs_sem,
    g_sem,
):
    pair = lax.axis_index("pair")
    ga = lax.axis_index("ga")
    c = pair % 2
    y = (pair // 2) % 4
    zh = (pair // 8) % 2
    x = pair // 16
    z = zh * 2 + ga

    def dev(dx=0, dy=0, dz=0, dc=0):
        xx, yy, zz, cc = (x + dx) % 4, (y + dy) % 4, (z + dz) % 4, (c + dc) % 2
        return {"pair": ((xx * 2 + zz // 2) * 4 + yy) * 2 + cc, "ga": zz % 2}

    core_peer = dev(dc=1)
    ga_peer = {"pair": pair, "ga": 1 - ga}
    others = [(e, f) for e in range(4) for f in range(2) if (e, f) != (0, 0)]
    peers = [core_peer] + [dev(dz=o) for o in (1, 2, 3)]
    for f in range(2):
        for e in (1, 2, 3):
            peers += [dev(dx=e, dz=2 * f), dev(dy=e, dz=2 * f)]

    def send(src, dst, device, s_sem, r_sem):
        pltpu.make_async_remote_copy(
            src_ref=src,
            dst_ref=dst,
            send_sem=s_sem,
            recv_sem=r_sem,
            device_id=device,
            device_id_type=MESH,
        ).start()

    def wait(ref, sem):
        pltpu.make_async_copy(ref, ref, sem).wait()

    S_PART, S_A, S_BCORE, S_BGA, S_ONE, S_TWO, S_Z, S_G1, S_G2, S_RELAY, S_FWD = (send_sem.at[i] for i in range(11))
    R_PART, R_Z = g_sem.at[0], g_sem.at[1]

    barrier = pltpu.get_barrier_semaphore()
    for peer in peers:
        pl.semaphore_signal(barrier, inc=1, device_id=peer, device_id_type=MESH)

    ld_win = pltpu.make_async_copy(pm_hbm.at[0, 0], win_buf, load_sem.at[0])
    ld_cl = pltpu.make_async_copy(cl_hbm, cl_buf, load_sem.at[1])
    ld_pv = pltpu.make_async_copy(pv_hbm, pv_buf, load_sem.at[2])
    ld_a = pltpu.make_async_copy(pm_hbm.at[:, :, :, c], a_buf.at[c], load_sem.at[3])
    ld_pc = pltpu.make_async_copy(pc_hbm, pc_buf, load_sem.at[4])
    ld_w = [
        pltpu.make_async_copy(w_hbm.at[pl.ds(k * 2048, 2048)], w_buf.at[pl.ds(k * 2048, 2048)], load_sem.at[5 + k])
        for k in range(4)
    ]

    @pl.when(ga == 0)
    def _():
        ld_win.start()

    ld_cl.start()
    ld_pv.start()
    for copy in ld_w:
        copy.start()
    ld_a.start()

    ld_cl.wait()

    @pl.when(ga == 0)
    def _():
        ld_win.wait()
        v = cl_buf[...]
        for n in range(CHUNKS):
            rows = win_buf[n].reshape(W, KB)
            b_buf[c, n] = (rows.astype(F32) * v).astype(BF)

    ld_pv.wait()
    part = None
    for k in range(4):
        ld_w[k].wait()
        term = jnp.dot(
            pv_buf[:, k * 2048 : (k + 1) * 2048],
            w_buf[k * 2048 : (k + 1) * 2048, :],
            preferred_element_type=F32,
        )
        part = term if part is None else part + term
    part_buf[...] = part.reshape(2, 32, KB)

    pl.semaphore_wait(barrier, len(peers))

    send(part_buf.at[1 - ga], part_recv, ga_peer, S_PART, R_PART)

    def b_to_core(n):
        send(b_buf.at[c, n], b_buf.at[c, n], core_peer, S_BCORE, b_sem.at[0, n])

    def b_wait(n):
        wait(b_buf.at[1 - c, n], b_sem.at[0, n])

    def a_to_core(r):
        rows = pl.ds(r * 32, 32)
        send(pm_hbm.at[:, :, :, 1 - c, rows], a_buf.at[c, :, :, :, rows], core_peer, S_A, b_sem.at[2, r])

    def a_wait(r):
        wait(a_buf.at[1 - c, :, :, :, pl.ds(r * 32, 32)], b_sem.at[2, r])

    @pl.when(ga == 0)
    def _():
        for n in range(CHUNKS):
            send(b_buf.at[c, n], b_buf.at[c, n], ga_peer, S_BGA, b_sem.at[1, n])
        for n in range(CHUNKS):
            b_to_core(n)

    for r in range(2):
        a_to_core(r)

    def tile_rows(s, r, d, h):
        rows = pl.ds(r * 32, 32)
        if r == 0:
            value = a_buf[s, (x + d) % 4, h, :, rows, :]
        else:
            value = a_buf[s, :, h, (y + d) % 4, rows, :]
        return value.reshape(128, KB)

    def tile(r, n, parts):
        total = None
        for s in range(2):
            rows = jnp.concatenate([tile_rows(s, r, d, h) for d, h in parts], axis=0)
            term = dot_t(rows, b_buf[s, n])
            total = term if total is None else total + term
        return total.reshape(len(parts), 4, 32, W)

    def first(r, way):
        d = 1 if way == 0 else 3
        return dev(dx=d) if r == 0 else dev(dy=d)

    def second(r, e, f):
        return dev(dy=e, dz=2 * f) if r == 0 else dev(dx=e, dz=2 * f)

    def rs_opp(r, n):
        snd1[r, n, 0] = tile(r, n, ((2, 0), (2, 1))).astype(BF)
        for way in range(2):
            send(snd1.at[r, n, 0, way], opp_recv.at[r, n, way], first(r, way), S_ONE, rs_sem.at[0, r, n])

    def rs_dir(r, n):
        snd1[r, n, 1] = tile(r, n, ((1, 1), (3, 0))).astype(BF)
        for way in range(2):
            send(snd1.at[r, n, 1, way], near_recv.at[r, n, way], first(r, way), S_ONE, rs_sem.at[1, r, n])

    def rs_comb(n):
        for r in range(2):
            own = tile(r, n, ((1, 0), (3, 1)))
            wait(opp_recv.at[r, n], rs_sem.at[0, r, n])
            for way in range(2):
                snd1[r, n, 2, way] = (own[way] + opp_recv[r, n, way].astype(F32)).astype(BF)
                send(snd1.at[r, n, 2, way], near_recv.at[r, n, 2 + way], first(r, way), S_ONE, rs_sem.at[1, r, n])
        for r in range(2):
            acc1[r, n] = tile(r, n, ((0, 0), (0, 1)))

    def rs_second(n):
        for r in range(2):
            wait(near_recv.at[r, n], rs_sem.at[1, r, n])
            for h in range(2):
                acc1[r, n, h] = (
                    acc1[r, n, h] + near_recv[r, n, 1 - h].astype(F32) + near_recv[r, n, 2 + h].astype(F32)
                )
            me = y if r == 0 else x
            for k, (e, f) in enumerate(others):
                hh = zh if f == 0 else 1 - zh
                snd2[r, n, k] = acc1[r, n, hh, (me + e) % 4].astype(BF)
                send(snd2.at[r, n, k], recv2.at[r, n, k], second(r, e, f), S_TWO, rs_sem.at[2, r, n])

    def rs_last(n):
        for r in range(2):
            me = y if r == 0 else x
            total = acc1[r, n, zh, me]
            wait(recv2.at[r, n], rs_sem.at[2, r, n])
            for k in range(len(others)):
                total = total + recv2[r, n, k].astype(F32)
            exchange_ref[r * 32 : r * 32 + 32, n * W : n * W + W] = total

    def slab(h, d, e):
        if h == 0:
            return img.at[c, h, (x + d) % 4, (y + e) % 4]
        return img.at[c, h, (x + e) % 4, (y + d) % 4]

    def line(cc, h, e):
        return img.at[cc, h, :, (y + e) % 4] if h == 0 else img.at[cc, h, (x + e) % 4]

    def along(h, d):
        return dev(dx=d) if h == 0 else dev(dy=d)

    def across(h, e):
        return dev(dy=e) if h == 0 else dev(dx=e)

    def g2_sem(h, e, late):
        return g_sem.at[4 + h * 4 + (e // 2) * 2 + late]

    def slabs(n):
        return img.at[0, 0, 0, pl.ds(0, n)]

    def g_sum():
        wait(part_recv, R_PART)
        img[c, zh, x, y, ga] = (part_buf[ga] + part_recv[...]).astype(BF)
        mine = img.at[c, zh, x, y, ga]
        for f in (2, 1, 3):
            send(mine, mine, dev(dz=f), S_Z, R_Z)

    def g_second_send(h, d):
        for e in (1, 3):
            send(slab(h, d, 0), slab(h, d, 0), across(h, e), S_G2, g2_sem(h, 4 - e, 0 if d == 0 else 1))

    def g_first():
        wait(img.at[0, 0, 0, pl.ds(0, 3), 0], R_Z)
        for h in range(2):
            for d in (2, 1, 3):
                send(slab(h, 0, 0), slab(h, 0, 0), along(h, d), S_G1, g_sem.at[2 + h])
        for h in range(2):
            g_second_send(h, 0)

    def g_second():
        for h in range(2):
            wait(slabs(3), g_sem.at[2 + h])
            for d in (1, 3, 2):
                g_second_send(h, d)
        for h in range(2):
            g_forward(h, 0)

    def g_relay_send(h, d):
        e = 1 if d in (0, 2) else 3
        send(slab(h, d, 4 - e), slab(h, d, 4 - e), across(h, e), S_RELAY, g_sem.at[12 + h])

    def g_relay_own():
        for h in range(2):
            wait(slabs(1), g2_sem(h, 3, 0))
            g_relay_send(h, 0)

    def g_relay():
        for h in range(2):
            wait(slabs(3), g2_sem(h, 1, 1))
            for d in (1, 3):
                g_relay_send(h, d)
            wait(slabs(3), g2_sem(h, 3, 1))
            g_relay_send(h, 2)
            wait(slabs(1), g2_sem(h, 1, 0))

    def g_forward(h, e):
        send(line(c, h, e), line(c, h, e), core_peer, S_FWD, g_sem.at[14 + h * 4 + e])

    def g_forwarded(h, e):
        wait(line(1 - c, h, e), g_sem.at[14 + h * 4 + e])

    def g_last():
        for h in range(2):
            wait(slabs(4), g_sem.at[12 + h])
            g_forward(h, 2)

    def direct_group(cc, h, e, begin=False):
        total = None
        for j in range(4):
            xx, yy = (j, (y + e) % 4) if h == 0 else ((x + e) % 4, j)
            cols = pl.ds(pl.multiple_of((((xx * 2 + h) * 4 + yy) * 2 + cc) * KB, KB), KB)
            term = dot_t(pc_buf[:, cols], img[cc, h, xx, yy].reshape(64, KB))
            total = term if total is None else total + term
        dacc[...] = total if begin else dacc[...] + total

    def fetch(n):
        @pl.when(ga == 1)
        def _():
            wait(b_buf.at[c, n], b_sem.at[1, n])
            b_to_core(n)

    def open_late(n):
        @pl.when(ga == 1)
        def _():
            b_wait(n)
            for r in range(2):
                rs_opp(r, n)
            for r in range(2):
                rs_dir(r, n)

    ld_a.wait()
    a_wait(0)

    @pl.when(ga == 0)
    def _():
        for n in range(CHUNKS):
            b_wait(n)
            rs_opp(0, n)

    a_wait(1)
    ld_pc.start()

    @pl.when(ga == 0)
    def _():
        for n in range(CHUNKS):
            rs_opp(1, n)

    g_sum()

    @pl.when(ga == 0)
    def _():
        for n in range(CHUNKS):
            for r in range(2):
                rs_dir(r, n)

    fetch(0)
    fetch(1)
    open_late(0)
    g_first()
    fetch(2)
    open_late(1)
    fetch(3)
    rs_comb(0)
    open_late(2)
    g_second()
    open_late(3)
    rs_comb(1)
    g_relay_own()
    rs_comb(2)
    rs_second(0)
    g_relay()
    for h in range(2):
        for e in (1, 3):
            g_forward(h, e)
    rs_comb(3)
    rs_second(1)
    ld_pc.wait()
    for h in range(2):
        direct_group(c, h, 0, begin=h == 0)
    for h in range(2):
        g_forwarded(h, 0)
        direct_group(1 - c, h, 0)
    rs_second(2)
    g_last()
    rs_last(0)
    for h in range(2):
        for e in (1, 3):
            direct_group(c, h, e)
    rs_second(3)
    rs_last(1)
    for h in range(2):
        for e in (1, 3):
            g_forwarded(h, e)
            direct_group(1 - c, h, e)
    rs_last(2)
    for h in range(2):
        direct_group(c, h, 2)
        g_forwarded(h, 2)
        direct_group(1 - c, h, 2)
    direct_ref[...] = dacc[...].T
    rs_last(3)

    wait(part_recv, S_PART)
    wait(a_buf.at[0], S_A)
    wait(b_buf.at[0], S_BCORE)

    @pl.when(ga == 0)
    def _():
        wait(b_buf.at[0], S_BGA)

    wait(snd1, S_ONE)
    wait(snd2, S_TWO)
    wait(img.at[0, 0, 0, pl.ds(0, 3), 0], S_Z)
    wait(img.at[0, 0, pl.ds(0, 2), pl.ds(0, 3)], S_G1)
    wait(img.at[0, 0], S_G2)
    wait(img.at[0, 0, pl.ds(0, 2)], S_RELAY)
    wait(img.at[0], S_FWD)


def write_out(a_ref, b_ref, a_out, b_out):
    a_out[...] = a_ref[...]
    b_out[...] = b_ref[...]


def solution(mesh):
    def local(pair_valence, screened, pair_conduction, pair_mixed, coulomb):
        anywhere = pl.BlockSpec(memory_space=pl.ANY)
        vmem = pl.BlockSpec(memory_space=pltpu.VMEM)
        shapes = (jax.ShapeDtypeStruct((64, 512), F32), jax.ShapeDtypeStruct((64, 512), F32))
        direct, exchange = pl.pallas_call(
            kernel,
            out_shape=shapes,
            in_specs=[anywhere] * 5,
            out_specs=(vmem, vmem),
            scratch_shapes=[
                pltpu.VMEM((64, 8192), BF),
                pltpu.VMEM((8192, KB), BF),
                pltpu.VMEM((512, 16384), BF),
                pltpu.VMEM((2, 4, 2, 4, 64, KB), BF),
                pltpu.VMEM((2, CHUNKS, W, KB), BF),
                pltpu.VMEM((4, 2, 64, KB), BF),
                pltpu.VMEM((1, KB), F32),
                pltpu.VMEM((2, 32, KB), F32),
                pltpu.VMEM((32, KB), F32),
                pltpu.VMEM((2, 2, 4, 4, 2, 32, KB), BF),
                pltpu.VMEM((2, CHUNKS, 3, 2, 4, 32, W), BF),
                pltpu.VMEM((2, CHUNKS, 2, 4, 32, W), BF),
                pltpu.VMEM((2, CHUNKS, 4, 4, 32, W), BF),
                pltpu.VMEM((2, CHUNKS, 2, 4, 32, W), F32),
                pltpu.VMEM((2, CHUNKS, 7, 32, W), BF),
                pltpu.VMEM((2, CHUNKS, 7, 32, W), BF),
                pltpu.VMEM((512, 64), F32),
                pltpu.SemaphoreType.DMA((9,)),
                pltpu.SemaphoreType.DMA((11,)),
                pltpu.SemaphoreType.DMA((3, CHUNKS)),
                pltpu.SemaphoreType.DMA((3, 2, CHUNKS)),
                pltpu.SemaphoreType.DMA((22,)),
            ],
            compiler_params=pltpu.CompilerParams(
                collective_id=0, has_side_effects=True, vmem_limit_bytes=60 << 20
            ),
            cost_estimate=pl.CostEstimate(flops=3 << 30, bytes_accessed=24 << 20, transcendentals=0),
        )(
            pair_valence,
            screened,
            pair_conduction,
            pair_mixed.reshape(4, 2, 4, 2, 64, KB),
            coulomb.reshape(1, KB),
        )
        direct, exchange = pl.pallas_call(write_out, out_shape=shapes)(direct, exchange)
        return direct.T, exchange

    return jax.shard_map(
        local,
        mesh=mesh,
        in_specs=(
            P(None, "ga"),
            P("ga", "pair"),
            P(("pair", "ga"), None),
            P("ga", "pair"),
            P("pair"),
        ),
        out_specs=(P(("pair", "ga"), None), P(("ga", "pair"), None)),
        check_vma=False,
    )
```

```python
import jax
import jax.numpy as jnp
from jax import lax
from jax.experimental import pallas as pl
from jax.experimental.pallas import tpu as pltpu
from jax.sharding import PartitionSpec as P

MESH = pl.DeviceIdType.MESH
BF = jnp.bfloat16
F32 = jnp.float32
KB = 256
CHUNKS = 4
W = 512 // CHUNKS


def dot_t(a, b):
    return lax.dot_general(a, b, (((1,), (1,)), ((), ())), preferred_element_type=F32)


def kernel(
    pv_hbm,
    w_hbm,
    pc_hbm,
    pm_hbm,
    cl_hbm,
    direct_ref,
    exchange_ref,
    pv_buf,
    w_buf,
    pc_buf,
    a_buf,
    b_buf,
    win_buf,
    cl_buf,
    part_buf,
    part_recv,
    img,
    snd1,
    opp_recv,
    near_recv,
    acc1,
    snd2,
    recv2,
    dacc,
    load_sem,
    send_sem,
    b_sem,
    rs_sem,
    g_sem,
):
    pair = lax.axis_index("pair")
    ga = lax.axis_index("ga")
    c = pair % 2
    y = (pair // 2) % 4
    zh = (pair // 8) % 2
    x = pair // 16
    z = zh * 2 + ga

    def dev(dx=0, dy=0, dz=0, dc=0):
        xx, yy, zz, cc = (x + dx) % 4, (y + dy) % 4, (z + dz) % 4, (c + dc) % 2
        return {"pair": ((xx * 2 + zz // 2) * 4 + yy) * 2 + cc, "ga": zz % 2}

    core_peer = dev(dc=1)
    ga_peer = {"pair": pair, "ga": 1 - ga}
    others = [(e, f) for e in range(4) for f in range(2) if (e, f) != (0, 0)]
    peers = [core_peer] + [dev(dz=o) for o in (1, 2, 3)]
    for f in range(2):
        for e in (1, 2, 3):
            peers += [dev(dx=e, dz=2 * f), dev(dy=e, dz=2 * f)]
    peers += [dev(dx=d, dy=e) for d in (1, 2, 3) for e in (1, 2, 3)]

    def send(src, dst, device, s_sem, r_sem):
        pltpu.make_async_remote_copy(
            src_ref=src,
            dst_ref=dst,
            send_sem=s_sem,
            recv_sem=r_sem,
            device_id=device,
            device_id_type=MESH,
        ).start()

    def wait(ref, sem):
        pltpu.make_async_copy(ref, ref, sem).wait()

    S_PART, S_A, S_BCORE, S_BGA, S_ONE, S_TWO, S_Z, S_G1, S_G2, S_FWD = (send_sem.at[i] for i in range(10))
    R_PART, R_Z = g_sem.at[0], g_sem.at[1]

    barrier = pltpu.get_barrier_semaphore()
    for peer in peers:
        pl.semaphore_signal(barrier, inc=1, device_id=peer, device_id_type=MESH)

    ld_win = pltpu.make_async_copy(pm_hbm.at[0, 0], win_buf, load_sem.at[0])
    ld_cl = pltpu.make_async_copy(cl_hbm, cl_buf, load_sem.at[1])
    ld_pv = pltpu.make_async_copy(pv_hbm, pv_buf, load_sem.at[2])
    ld_a = pltpu.make_async_copy(pm_hbm.at[:, :, :, c], a_buf.at[c], load_sem.at[3])
    ld_pc = pltpu.make_async_copy(pc_hbm, pc_buf, load_sem.at[4])
    ld_w = [
        pltpu.make_async_copy(w_hbm.at[pl.ds(k * 2048, 2048)], w_buf.at[pl.ds(k * 2048, 2048)], load_sem.at[5 + k])
        for k in range(4)
    ]

    @pl.when(ga == 0)
    def _():
        ld_win.start()

    ld_cl.start()
    ld_pv.start()
    for copy in ld_w:
        copy.start()
    ld_a.start()

    ld_cl.wait()

    @pl.when(ga == 0)
    def _():
        ld_win.wait()
        v = cl_buf[...]
        for n in range(CHUNKS):
            rows = win_buf[n].reshape(W, KB)
            b_buf[c, n] = (rows.astype(F32) * v).astype(BF)

    ld_pv.wait()
    part = None
    for k in range(4):
        ld_w[k].wait()
        term = jnp.dot(
            pv_buf[:, k * 2048 : (k + 1) * 2048],
            w_buf[k * 2048 : (k + 1) * 2048, :],
            preferred_element_type=F32,
        )
        part = term if part is None else part + term
    part_buf[...] = part.reshape(2, 32, KB)

    pl.semaphore_wait(barrier, len(peers))

    send(part_buf.at[1 - ga], part_recv, ga_peer, S_PART, R_PART)

    def b_to_core(n):
        send(b_buf.at[c, n], b_buf.at[c, n], core_peer, S_BCORE, b_sem.at[0, n])

    def b_to_ga(n):
        send(b_buf.at[c, n], b_buf.at[c, n], ga_peer, S_BGA, b_sem.at[1, n])

    def b_wait(n):
        wait(b_buf.at[1 - c, n], b_sem.at[0, n])

    def a_to_core(r, d):
        rows = pl.ds(r * 32, 32)
        if r == 0:
            src, dst = pm_hbm.at[(x + d) % 4, :, :, 1 - c, rows], a_buf.at[c, (x + d) % 4, :, :, rows]
        else:
            src, dst = pm_hbm.at[:, :, (y + d) % 4, 1 - c, rows], a_buf.at[c, :, :, (y + d) % 4, rows]
        send(src, dst, core_peer, S_A, b_sem.at[2 + r, d])

    def a_wait(r, d):
        wait(a_buf.at[1 - c, 0, :, :, pl.ds(0, 32)], b_sem.at[2 + r, d])

    @pl.when(ga == 0)
    def _():
        for n in (0, 1):
            b_to_ga(n)
        for n in range(CHUNKS):
            b_to_core(n)

    for d in (2, 1, 3, 0):
        for r in range(2):
            a_to_core(r, d)

    def tile_rows(s, r, d, h):
        rows = pl.ds(r * 32, 32)
        if r == 0:
            value = a_buf[s, (x + d) % 4, h, :, rows, :]
        else:
            value = a_buf[s, :, h, (y + d) % 4, rows, :]
        return value.reshape(128, KB)

    def tile(r, n, parts):
        total = None
        for s in range(2):
            rows = jnp.concatenate([tile_rows(s, r, d, h) for d, h in parts], axis=0)
            term = dot_t(rows, b_buf[s, n])
            total = term if total is None else total + term
        return total.reshape(len(parts), 4, 32, W)

    def first(r, way):
        d = 1 if way == 0 else 3
        return dev(dx=d) if r == 0 else dev(dy=d)

    def second(r, e, f):
        return dev(dy=e, dz=2 * f) if r == 0 else dev(dx=e, dz=2 * f)

    def rs_opp(r, n):
        snd1[r, n, 0] = tile(r, n, ((2, 0), (2, 1))).astype(BF)
        for way in range(2):
            send(snd1.at[r, n, 0, way], opp_recv.at[r, n, way], first(r, way), S_ONE, rs_sem.at[0, r, n])

    def rs_dir(r, n):
        snd1[r, n, 1] = tile(r, n, ((1, 1), (3, 0))).astype(BF)
        for way in range(2):
            send(snd1.at[r, n, 1, way], near_recv.at[r, n, way], first(r, way), S_ONE, rs_sem.at[1, r, n])

    def rs_comb(n):
        for r in range(2):
            own = tile(r, n, ((1, 0), (3, 1)))
            wait(opp_recv.at[r, n], rs_sem.at[0, r, n])
            for way in range(2):
                snd1[r, n, 2, way] = (own[way] + opp_recv[r, n, way].astype(F32)).astype(BF)
                send(snd1.at[r, n, 2, way], near_recv.at[r, n, 2 + way], first(r, way), S_ONE, rs_sem.at[1, r, n])
        for r in range(2):
            acc1[r, n] = tile(r, n, ((0, 0), (0, 1)))

    def rs_second(n):
        for r in range(2):
            wait(near_recv.at[r, n], rs_sem.at[1, r, n])
            for h in range(2):
                acc1[r, n, h] = (
                    acc1[r, n, h] + near_recv[r, n, 1 - h].astype(F32) + near_recv[r, n, 2 + h].astype(F32)
                )
            me = y if r == 0 else x
            for k, (e, f) in enumerate(others):
                hh = zh if f == 0 else 1 - zh
                snd2[r, n, k] = acc1[r, n, hh, (me + e) % 4].astype(BF)
                send(snd2.at[r, n, k], recv2.at[r, n, k], second(r, e, f), S_TWO, rs_sem.at[2, r, n])

    def rs_last(n):
        for r in range(2):
            me = y if r == 0 else x
            total = acc1[r, n, zh, me]
            wait(recv2.at[r, n], rs_sem.at[2, r, n])
            for k in range(len(others)):
                total = total + recv2[r, n, k].astype(F32)
            exchange_ref[r * 32 : r * 32 + 32, n * W : n * W + W] = total

    def slab(h, d, e):
        if h == 0:
            return img.at[0, h, (x + d) % 4, (y + e) % 4]
        return img.at[0, h, (x + e) % 4, (y + d) % 4]

    def line(h, e):
        return img.at[0, h, :, (y + e) % 4] if h == 0 else img.at[0, h, (x + e) % 4]

    def row(d):
        return img.at[1, zh, (x + d) % 4, :, ga]

    def along(h, d):
        return dev(dx=d) if h == 0 else dev(dy=d)

    def across(h, e):
        return dev(dy=e) if h == 0 else dev(dx=e)

    def slabs(n):
        return img.at[0, 0, 0, pl.ds(0, n)]

    def g_sum():
        wait(part_recv, R_PART)
        img[c, zh, x, y, ga] = (part_buf[ga] + part_recv[...]).astype(BF)

        @pl.when(c == 0)
        def _():
            mine = img.at[0, zh, x, y, ga]
            for f in (2, 1, 3):
                send(mine, mine, dev(dz=f), S_Z, R_Z)

        @pl.when(c == 1)
        def _():
            mine = img.at[1, zh, x, y, ga]
            for d in (0, 2, 1, 3):
                for e in (0, 2, 1, 3):
                    if (d, e) != (0, 0):
                        send(mine, mine, dev(dx=d, dy=e), S_G1, g_sem.at[2 + (4 - d) % 4])

    def g_second_send(h, d):
        for e in (2, 1, 3):
            send(slab(h, d, 0), slab(h, d, 0), across(h, e), S_G2, g_sem.at[4 + h * 4 + 4 - e])

    def g_first():
        @pl.when(c == 0)
        def _():
            wait(img.at[0, 0, 0, pl.ds(0, 3), 0], R_Z)
            for h in range(2):
                for d in (2, 1, 3):
                    send(slab(h, 0, 0), slab(h, 0, 0), along(h, d), S_G1, g_sem.at[2 + h])
            for h in range(2):
                g_second_send(h, 0)

        @pl.when(c == 1)
        def _():
            for d in (0, 1, 3, 2):
                wait(img.at[0, 0, 0, pl.ds(0, 4 if d else 3), 0], g_sem.at[2 + d])
                for f in (2, 1, 3):
                    send(row(d), row(d), dev(dz=f), S_Z, g_sem.at[6 + f])
            p_forward(0)

    def g_second():
        @pl.when(c == 0)
        def _():
            for h in range(2):
                wait(slabs(3), g_sem.at[2 + h])
                for d in (1, 3, 2):
                    g_second_send(h, d)
            for h in range(2):
                g_forward(h, 0)

    def g_lines():
        @pl.when(c == 0)
        def _():
            for e in (1, 3):
                for h in range(2):
                    wait(slabs(4), g_sem.at[4 + h * 4 + e])
                    g_forward(h, e)

    def plane(f):
        zz = (z + f) % 4
        return img.at[1, zz // 2, :, :, zz % 2]

    def g_forward(h, e):
        send(line(h, e), line(h, e), core_peer, S_FWD, g_sem.at[14 + h * 4 + e])

    def p_forward(f):
        send(plane(f), plane(f), core_peer, S_FWD, g_sem.at[14 + f])

    def g_last():
        @pl.when(c == 0)
        def _():
            for h in range(2):
                wait(slabs(4), g_sem.at[4 + h * 4 + 2])
                g_forward(h, 2)

    def p_last():
        @pl.when(c == 1)
        def _():
            for f in (1, 3, 2):
                wait(img.at[1, 0, :, :, 0], g_sem.at[6 + (4 - f)])
                p_forward(f)

    def direct_group(cc, h, e, begin=False):
        total = None
        for j in range(4):
            xx, yy = (j, (y + e) % 4) if h == 0 else ((x + e) % 4, j)
            cols = pl.ds(pl.multiple_of((((xx * 2 + h) * 4 + yy) * 2 + cc) * KB, KB), KB)
            term = dot_t(pc_buf[:, cols], img[cc, h, xx, yy].reshape(64, KB))
            total = term if total is None else total + term
        dacc[...] = total if begin else dacc[...] + total

    def first_direct(e, begin=False):
        @pl.when(c == 1)
        def _():
            for h in range(2):
                wait(line(h, e), g_sem.at[14 + h * 4 + e])

        for h in range(2):
            direct_group(0, h, e, begin and h == 0)

    def second_direct(es):
        for h in range(2):
            for e in es:
                direct_group(1, h, e)

    def fetch(n):
        @pl.when(ga == 1)
        def _():
            wait(b_buf.at[c, n], b_sem.at[1, n])
            b_to_core(n)

    def open_late(n):
        @pl.when(ga == 1)
        def _():
            b_wait(n)
            for r in range(2):
                rs_opp(r, n)
            for r in range(2):
                rs_dir(r, n)

    ld_a.wait()
    for r in range(2):
        a_wait(r, 2)

    @pl.when(ga == 0)
    def _():
        for n in range(CHUNKS):
            b_wait(n)
            for r in range(2):
                rs_opp(r, n)

    g_sum()

    @pl.when(ga == 0)
    def _():
        for n in (2, 3):
            b_to_ga(n)

    for d in (1, 3, 0):
        for r in range(2):
            a_wait(r, d)
    ld_pc.start()

    @pl.when(ga == 0)
    def _():
        for n in range(CHUNKS):
            for r in range(2):
                rs_dir(r, n)

    fetch(0)
    fetch(1)
    open_late(0)
    g_first()
    fetch(2)
    open_late(1)
    fetch(3)
    open_late(2)
    rs_comb(0)
    open_late(3)
    rs_comb(1)
    rs_comb(2)
    g_second()
    rs_comb(3)
    rs_second(0)
    rs_second(1)
    p_last()
    ld_pc.wait()
    first_direct(0, True)
    rs_second(2)
    g_lines()
    rs_second(3)

    @pl.when(c == 0)
    def _():
        for f in range(4):
            wait(img.at[1, 0, :, :, 0], g_sem.at[14 + f])

    second_direct((0, 1))
    rs_last(0)
    second_direct((2, 3))
    rs_last(1)
    g_last()
    for e in (1, 3):
        first_direct(e)
    rs_last(2)
    first_direct(2)
    direct_ref[...] = dacc[...].T
    rs_last(3)

    wait(part_recv, S_PART)
    wait(a_buf.at[0], S_A)
    wait(b_buf.at[0], S_BCORE)

    @pl.when(ga == 0)
    def _():
        wait(b_buf.at[0], S_BGA)

    wait(snd1, S_ONE)
    wait(snd2, S_TWO)

    @pl.when(c == 0)
    def _():
        wait(img.at[0, 0, 0, pl.ds(0, 3), 0], S_Z)
        wait(img.at[0, 0, pl.ds(0, 2), pl.ds(0, 3)], S_G1)
        wait(img.at[0, :, pl.ds(0, 3)], S_G2)

    @pl.when(c == 1)
    def _():
        wait(img.at[0, :, :, pl.ds(0, 3)], S_Z)
        wait(pc_buf.at[pl.ds(0, 16), pl.ds(0, 15 * 512)], S_G1)

    wait(img.at[0], S_FWD)


def write_out(a_ref, b_ref, a_out, b_out):
    a_out[...] = a_ref[...]
    b_out[...] = b_ref[...]


def solution(mesh):
    def local(pair_valence, screened, pair_conduction, pair_mixed, coulomb):
        anywhere = pl.BlockSpec(memory_space=pl.ANY)
        vmem = pl.BlockSpec(memory_space=pltpu.VMEM)
        shapes = (jax.ShapeDtypeStruct((64, 512), F32), jax.ShapeDtypeStruct((64, 512), F32))
        direct, exchange = pl.pallas_call(
            kernel,
            out_shape=shapes,
            in_specs=[anywhere] * 5,
            out_specs=(vmem, vmem),
            scratch_shapes=[
                pltpu.VMEM((64, 8192), BF),
                pltpu.VMEM((8192, KB), BF),
                pltpu.VMEM((512, 16384), BF),
                pltpu.VMEM((2, 4, 2, 4, 64, KB), BF),
                pltpu.VMEM((2, CHUNKS, W, KB), BF),
                pltpu.VMEM((4, 2, 64, KB), BF),
                pltpu.VMEM((1, KB), F32),
                pltpu.VMEM((2, 32, KB), F32),
                pltpu.VMEM((32, KB), F32),
                pltpu.VMEM((2, 2, 4, 4, 2, 32, KB), BF),
                pltpu.VMEM((2, CHUNKS, 3, 2, 4, 32, W), BF),
                pltpu.VMEM((2, CHUNKS, 2, 4, 32, W), BF),
                pltpu.VMEM((2, CHUNKS, 4, 4, 32, W), BF),
                pltpu.VMEM((2, CHUNKS, 2, 4, 32, W), F32),
                pltpu.VMEM((2, CHUNKS, 7, 32, W), BF),
                pltpu.VMEM((2, CHUNKS, 7, 32, W), BF),
                pltpu.VMEM((512, 64), F32),
                pltpu.SemaphoreType.DMA((9,)),
                pltpu.SemaphoreType.DMA((10,)),
                pltpu.SemaphoreType.DMA((4, CHUNKS)),
                pltpu.SemaphoreType.DMA((3, 2, CHUNKS)),
                pltpu.SemaphoreType.DMA((22,)),
            ],
            compiler_params=pltpu.CompilerParams(
                collective_id=0, has_side_effects=True, vmem_limit_bytes=60 << 20
            ),
            cost_estimate=pl.CostEstimate(flops=3 << 30, bytes_accessed=24 << 20, transcendentals=0),
        )(
            pair_valence,
            screened,
            pair_conduction,
            pair_mixed.reshape(4, 2, 4, 2, 64, KB),
            coulomb.reshape(1, KB),
        )
        direct, exchange = pl.pallas_call(write_out, out_shape=shapes)(direct, exchange)
        return direct.T, exchange

    return jax.shard_map(
        local,
        mesh=mesh,
        in_specs=(
            P(None, "ga"),
            P("ga", "pair"),
            P(("pair", "ga"), None),
            P("ga", "pair"),
            P("pair"),
        ),
        out_specs=(P(("pair", "ga"), None), P(("ga", "pair"), None)),
        check_vma=False,
    )
```

```python
import jax
import jax.numpy as jnp
from jax import lax
from jax.experimental import pallas as pl
from jax.experimental.pallas import tpu as pltpu
from jax.sharding import PartitionSpec as P

MESH = pl.DeviceIdType.MESH
BF = jnp.bfloat16
F32 = jnp.float32
KB = 256
CHUNKS = 4
W = 512 // CHUNKS


def dot_t(a, b):
    return lax.dot_general(a, b, (((1,), (1,)), ((), ())), preferred_element_type=F32)


def kernel(
    pv_hbm,
    w_hbm,
    pc_hbm,
    pm_hbm,
    cl_hbm,
    direct_ref,
    exchange_ref,
    pv_buf,
    w_buf,
    pc_buf,
    a_buf,
    b_buf,
    win_buf,
    cl_buf,
    part_buf,
    part_recv,
    img,
    snd1,
    opp_recv,
    near_recv,
    acc1,
    snd2,
    recv2,
    dacc,
    load_sem,
    send_sem,
    b_sem,
    rs_sem,
    g_sem,
):
    pair = lax.axis_index("pair")
    ga = lax.axis_index("ga")
    c = pair % 2
    y = (pair // 2) % 4
    zh = (pair // 8) % 2
    x = pair // 16
    z = zh * 2 + ga

    def dev(dx=0, dy=0, dz=0, dc=0):
        xx, yy, zz, cc = (x + dx) % 4, (y + dy) % 4, (z + dz) % 4, (c + dc) % 2
        return {"pair": ((xx * 2 + zz // 2) * 4 + yy) * 2 + cc, "ga": zz % 2}

    core_peer = dev(dc=1)
    ga_peer = {"pair": pair, "ga": 1 - ga}
    others = [(e, f) for e in range(4) for f in range(2) if (e, f) != (0, 0)]
    peers = [core_peer] + [dev(dz=o) for o in (1, 2, 3)]
    for f in range(2):
        for e in (1, 2, 3):
            peers += [dev(dx=e, dz=2 * f), dev(dy=e, dz=2 * f)]
    peers += [dev(dx=d, dy=e) for d in (1, 2, 3) for e in (1, 2, 3)]

    def send(src, dst, device, s_sem, r_sem):
        pltpu.make_async_remote_copy(
            src_ref=src,
            dst_ref=dst,
            send_sem=s_sem,
            recv_sem=r_sem,
            device_id=device,
            device_id_type=MESH,
        ).start()

    def wait(ref, sem):
        pltpu.make_async_copy(ref, ref, sem).wait()

    S_PART, S_A, S_BCORE, S_BGA, S_ONE, S_TWO, S_Z, S_G1, S_G2, S_FWD = (send_sem.at[i] for i in range(10))
    R_PART, R_Z = g_sem.at[0], g_sem.at[1]

    barrier = pltpu.get_barrier_semaphore()
    for peer in peers:
        pl.semaphore_signal(barrier, inc=1, device_id=peer, device_id_type=MESH)

    ld_win = pltpu.make_async_copy(pm_hbm.at[0, 0], win_buf, load_sem.at[0])
    ld_cl = pltpu.make_async_copy(cl_hbm, cl_buf, load_sem.at[1])
    ld_pv = pltpu.make_async_copy(pv_hbm, pv_buf, load_sem.at[2])
    ld_a = pltpu.make_async_copy(pm_hbm.at[:, :, :, c], a_buf.at[c], load_sem.at[3])
    ld_pc = pltpu.make_async_copy(pc_hbm, pc_buf, load_sem.at[4])
    ld_w = [
        pltpu.make_async_copy(w_hbm.at[pl.ds(k * 2048, 2048)], w_buf.at[pl.ds(k * 2048, 2048)], load_sem.at[5 + k])
        for k in range(4)
    ]

    @pl.when(ga == 0)
    def _():
        ld_win.start()

    ld_cl.start()
    ld_pv.start()
    for copy in ld_w:
        copy.start()
    ld_a.start()

    ld_cl.wait()

    @pl.when(ga == 0)
    def _():
        ld_win.wait()
        v = cl_buf[...]
        for n in range(CHUNKS):
            rows = win_buf[n].reshape(W, KB)
            b_buf[c, n] = (rows.astype(F32) * v).astype(BF)

    ld_pv.wait()
    part = None
    for k in range(4):
        ld_w[k].wait()
        term = jnp.dot(
            pv_buf[:, k * 2048 : (k + 1) * 2048],
            w_buf[k * 2048 : (k + 1) * 2048, :],
            preferred_element_type=F32,
        )
        part = term if part is None else part + term
    part_buf[...] = part.reshape(2, 32, KB)

    pl.semaphore_wait(barrier, len(peers))

    send(part_buf.at[1 - ga], part_recv, ga_peer, S_PART, R_PART)

    def b_to_core(n):
        send(b_buf.at[c, n], b_buf.at[c, n], core_peer, S_BCORE, b_sem.at[0, n])

    def b_to_ga(n):
        send(b_buf.at[c, n], b_buf.at[c, n], ga_peer, S_BGA, b_sem.at[1, n])

    def b_wait(n):
        wait(b_buf.at[1 - c, n], b_sem.at[0, n])

    def a_to_core(r, d):
        rows = pl.ds(r * 32, 32)
        if r == 0:
            src, dst = pm_hbm.at[(x + d) % 4, :, :, 1 - c, rows], a_buf.at[c, (x + d) % 4, :, :, rows]
        else:
            src, dst = pm_hbm.at[:, :, (y + d) % 4, 1 - c, rows], a_buf.at[c, :, :, (y + d) % 4, rows]
        send(src, dst, core_peer, S_A, b_sem.at[2 + r, d])

    def a_wait(r, d):
        wait(a_buf.at[1 - c, 0, :, :, pl.ds(0, 32)], b_sem.at[2 + r, d])

    @pl.when(ga == 0)
    def _():
        for n in (0, 1):
            b_to_ga(n)
        for n in range(CHUNKS):
            b_to_core(n)

    for d in (2, 1, 3, 0):
        for r in range(2):
            a_to_core(r, d)

    def tile_rows(s, r, d, h):
        rows = pl.ds(r * 32, 32)
        if r == 0:
            value = a_buf[s, (x + d) % 4, h, :, rows, :]
        else:
            value = a_buf[s, :, h, (y + d) % 4, rows, :]
        return value.reshape(128, KB)

    def tile(r, n, parts):
        total = None
        for s in range(2):
            rows = jnp.concatenate([tile_rows(s, r, d, h) for d, h in parts], axis=0)
            term = dot_t(rows, b_buf[s, n])
            total = term if total is None else total + term
        return total.reshape(len(parts), 4, 32, W)

    def first(r, way):
        d = 1 if way == 0 else 3
        return dev(dx=d) if r == 0 else dev(dy=d)

    def second(r, e, f):
        return dev(dy=e, dz=2 * f) if r == 0 else dev(dx=e, dz=2 * f)

    def rs_opp(r, n):
        snd1[r, n, 0] = tile(r, n, ((2, 0), (2, 1))).astype(BF)
        for way in range(2):
            send(snd1.at[r, n, 0, way], opp_recv.at[r, n, way], first(r, way), S_ONE, rs_sem.at[0, r, n])

    def rs_dir(r, n):
        snd1[r, n, 1] = tile(r, n, ((1, 1), (3, 0))).astype(BF)
        for way in range(2):
            send(snd1.at[r, n, 1, way], near_recv.at[r, n, way], first(r, way), S_ONE, rs_sem.at[1, r, n])

    def rs_comb(n):
        for r in range(2):
            own = tile(r, n, ((1, 0), (3, 1)))
            wait(opp_recv.at[r, n], rs_sem.at[0, r, n])
            for way in range(2):
                snd1[r, n, 2, way] = (own[way] + opp_recv[r, n, way].astype(F32)).astype(BF)
                send(snd1.at[r, n, 2, way], near_recv.at[r, n, 2 + way], first(r, way), S_ONE, rs_sem.at[1, r, n])

    def rs_second(n):
        for r in range(2):
            own = tile(r, n, ((0, 0), (0, 1)))
            wait(near_recv.at[r, n], rs_sem.at[1, r, n])
            for h in range(2):
                acc1[r, n, h] = (
                    own[h] + near_recv[r, n, 1 - h].astype(F32) + near_recv[r, n, 2 + h].astype(F32)
                )
            me = y if r == 0 else x
            for k, (e, f) in enumerate(others):
                hh = zh if f == 0 else 1 - zh
                snd2[r, n, k] = acc1[r, n, hh, (me + e) % 4].astype(BF)
                send(snd2.at[r, n, k], recv2.at[r, n, k], second(r, e, f), S_TWO, rs_sem.at[2, r, n])

    def rs_last(n):
        for r in range(2):
            me = y if r == 0 else x
            total = acc1[r, n, zh, me]
            wait(recv2.at[r, n], rs_sem.at[2, r, n])
            for k in range(len(others)):
                total = total + recv2[r, n, k].astype(F32)
            exchange_ref[r * 32 : r * 32 + 32, n * W : n * W + W] = total

    def slab(h, d, e):
        if h == 0:
            return img.at[0, h, (x + d) % 4, (y + e) % 4]
        return img.at[0, h, (x + e) % 4, (y + d) % 4]

    def line(h, e):
        return img.at[0, h, :, (y + e) % 4] if h == 0 else img.at[0, h, (x + e) % 4]

    def row(d):
        return img.at[1, zh, (x + d) % 4, :, ga]

    def along(h, d):
        return dev(dx=d) if h == 0 else dev(dy=d)

    def across(h, e):
        return dev(dy=e) if h == 0 else dev(dx=e)

    def slabs(n):
        return img.at[0, 0, 0, pl.ds(0, n)]

    def g_sum():
        wait(part_recv, R_PART)
        img[c, zh, x, y, ga] = (part_buf[ga] + part_recv[...]).astype(BF)

        @pl.when(c == 0)
        def _():
            mine = img.at[0, zh, x, y, ga]
            for f in (2, 1, 3):
                send(mine, mine, dev(dz=f), S_Z, R_Z)

        @pl.when(c == 1)
        def _():
            mine = img.at[1, zh, x, y, ga]
            for d in (0, 2, 1, 3):
                for e in (0, 2, 1, 3):
                    if (d, e) != (0, 0):
                        send(mine, mine, dev(dx=d, dy=e), S_G1, g_sem.at[2 + (4 - d) % 4])

    def g_second_send(h, d):
        for e in (2, 1, 3):
            send(slab(h, d, 0), slab(h, d, 0), across(h, e), S_G2, g_sem.at[4 + h * 4 + 4 - e])

    def g_first():
        @pl.when(c == 0)
        def _():
            wait(img.at[0, 0, 0, pl.ds(0, 3), 0], R_Z)
            for h in range(2):
                for d in (2, 1, 3):
                    send(slab(h, 0, 0), slab(h, 0, 0), along(h, d), S_G1, g_sem.at[2 + h])
            for h in range(2):
                g_second_send(h, 0)

        @pl.when(c == 1)
        def _():
            for d in (0, 1, 3, 2):
                wait(img.at[0, 0, 0, pl.ds(0, 4 if d else 3), 0], g_sem.at[2 + d])
                for f in (2, 1, 3):
                    send(row(d), row(d), dev(dz=f), S_Z, g_sem.at[6 + f])
            p_forward(0)

    def g_second():
        @pl.when(c == 0)
        def _():
            for h in range(2):
                wait(slabs(3), g_sem.at[2 + h])
                for d in (1, 3, 2):
                    g_second_send(h, d)
            for h in range(2):
                g_forward(h, 0)

    def g_lines():
        @pl.when(c == 0)
        def _():
            for e in (1, 3):
                for h in range(2):
                    wait(slabs(4), g_sem.at[4 + h * 4 + e])
                    g_forward(h, e)

    def plane(f):
        zz = (z + f) % 4
        return img.at[1, zz // 2, :, :, zz % 2]

    def g_forward(h, e):
        send(line(h, e), line(h, e), core_peer, S_FWD, g_sem.at[14 + h * 4 + e])

    def p_forward(f):
        send(plane(f), plane(f), core_peer, S_FWD, g_sem.at[14 + f])

    def g_last():
        @pl.when(c == 0)
        def _():
            for h in range(2):
                wait(slabs(4), g_sem.at[4 + h * 4 + 2])
                g_forward(h, 2)

    def p_last():
        @pl.when(c == 1)
        def _():
            for f in (1, 3, 2):
                wait(img.at[1, 0, :, :, 0], g_sem.at[6 + (4 - f)])
                p_forward(f)

    def direct_group(cc, h, e, begin=False):
        dense, images = [], []
        for j in range(4):
            xx, yy = (j, (y + e) % 4) if h == 0 else ((x + e) % 4, j)
            dense.append(pc_buf[:, pl.ds(pl.multiple_of((((xx * 2 + h) * 4 + yy) * 2 + cc) * KB, KB), KB)])
            images.append(img[cc, h, xx, yy].reshape(64, KB))
        total = dot_t(jnp.concatenate(dense, axis=1), jnp.concatenate(images, axis=1))
        dacc[...] = total if begin else dacc[...] + total

    def first_direct(e, begin=False):
        @pl.when(c == 1)
        def _():
            for h in range(2):
                wait(line(h, e), g_sem.at[14 + h * 4 + e])

        for h in range(2):
            direct_group(0, h, e, begin and h == 0)

    def second_direct(es):
        for h in range(2):
            for e in es:
                direct_group(1, h, e)

    def fetch(n):
        @pl.when(ga == 1)
        def _():
            wait(b_buf.at[c, n], b_sem.at[1, n])
            b_to_core(n)

    def open_late(n):
        @pl.when(ga == 1)
        def _():
            b_wait(n)
            for r in range(2):
                rs_opp(r, n)
            for r in range(2):
                rs_dir(r, n)

    ld_a.wait()
    for r in range(2):
        a_wait(r, 2)

    @pl.when(ga == 0)
    def _():
        for n in range(CHUNKS):
            b_wait(n)
            for r in range(2):
                rs_opp(r, n)

    g_sum()

    @pl.when(ga == 0)
    def _():
        for n in (2, 3):
            b_to_ga(n)

    for d in (1, 3, 0):
        for r in range(2):
            a_wait(r, d)
    ld_pc.start()

    @pl.when(ga == 0)
    def _():
        for n in range(CHUNKS):
            for r in range(2):
                rs_dir(r, n)

    fetch(0)
    open_late(0)
    fetch(1)
    g_first()
    open_late(1)
    fetch(2)
    open_late(2)
    fetch(3)
    rs_comb(0)
    open_late(3)
    rs_comb(1)
    rs_comb(2)
    g_second()
    rs_comb(3)
    rs_second(0)
    rs_second(1)
    p_last()
    ld_pc.wait()
    first_direct(0, True)
    rs_second(2)
    g_lines()
    rs_second(3)

    @pl.when(c == 0)
    def _():
        for f in range(4):
            wait(img.at[1, 0, :, :, 0], g_sem.at[14 + f])

    second_direct((0, 1))
    rs_last(0)
    second_direct((2, 3))
    rs_last(1)
    g_last()
    for e in (1, 3):
        first_direct(e)
    rs_last(2)
    first_direct(2)
    direct_ref[...] = dacc[...].T
    rs_last(3)

    wait(part_recv, S_PART)
    wait(a_buf.at[0], S_A)
    wait(b_buf.at[0], S_BCORE)

    @pl.when(ga == 0)
    def _():
        wait(b_buf.at[0], S_BGA)

    wait(snd1, S_ONE)
    wait(snd2, S_TWO)

    @pl.when(c == 0)
    def _():
        wait(img.at[0, 0, 0, pl.ds(0, 3), 0], S_Z)
        wait(img.at[0, 0, pl.ds(0, 2), pl.ds(0, 3)], S_G1)
        wait(img.at[0, :, pl.ds(0, 3)], S_G2)

    @pl.when(c == 1)
    def _():
        wait(img.at[0, :, :, pl.ds(0, 3)], S_Z)
        wait(pc_buf.at[pl.ds(0, 16), pl.ds(0, 15 * 512)], S_G1)

    wait(img.at[0], S_FWD)


def write_out(a_ref, b_ref, a_out, b_out):
    a_out[...] = a_ref[...]
    b_out[...] = b_ref[...]


def solution(mesh):
    def local(pair_valence, screened, pair_conduction, pair_mixed, coulomb):
        anywhere = pl.BlockSpec(memory_space=pl.ANY)
        vmem = pl.BlockSpec(memory_space=pltpu.VMEM)
        shapes = (jax.ShapeDtypeStruct((64, 512), F32), jax.ShapeDtypeStruct((64, 512), F32))
        direct, exchange = pl.pallas_call(
            kernel,
            out_shape=shapes,
            in_specs=[anywhere] * 5,
            out_specs=(vmem, vmem),
            scratch_shapes=[
                pltpu.VMEM((64, 8192), BF),
                pltpu.VMEM((8192, KB), BF),
                pltpu.VMEM((512, 16384), BF),
                pltpu.VMEM((2, 4, 2, 4, 64, KB), BF),
                pltpu.VMEM((2, CHUNKS, W, KB), BF),
                pltpu.VMEM((4, 2, 64, KB), BF),
                pltpu.VMEM((1, KB), F32),
                pltpu.VMEM((2, 32, KB), F32),
                pltpu.VMEM((32, KB), F32),
                pltpu.VMEM((2, 2, 4, 4, 2, 32, KB), BF),
                pltpu.VMEM((2, CHUNKS, 3, 2, 4, 32, W), BF),
                pltpu.VMEM((2, CHUNKS, 2, 4, 32, W), BF),
                pltpu.VMEM((2, CHUNKS, 4, 4, 32, W), BF),
                pltpu.VMEM((2, CHUNKS, 2, 4, 32, W), F32),
                pltpu.VMEM((2, CHUNKS, 7, 32, W), BF),
                pltpu.VMEM((2, CHUNKS, 7, 32, W), BF),
                pltpu.VMEM((512, 64), F32),
                pltpu.SemaphoreType.DMA((9,)),
                pltpu.SemaphoreType.DMA((10,)),
                pltpu.SemaphoreType.DMA((4, CHUNKS)),
                pltpu.SemaphoreType.DMA((3, 2, CHUNKS)),
                pltpu.SemaphoreType.DMA((22,)),
            ],
            compiler_params=pltpu.CompilerParams(
                collective_id=0, has_side_effects=True, vmem_limit_bytes=60 << 20
            ),
            cost_estimate=pl.CostEstimate(flops=3 << 30, bytes_accessed=24 << 20, transcendentals=0),
        )(
            pair_valence,
            screened,
            pair_conduction,
            pair_mixed.reshape(4, 2, 4, 2, 64, KB),
            coulomb.reshape(1, KB),
        )
        direct, exchange = pl.pallas_call(write_out, out_shape=shapes)(direct, exchange)
        return direct.T, exchange

    return jax.shard_map(
        local,
        mesh=mesh,
        in_specs=(
            P(None, "ga"),
            P("ga", "pair"),
            P(("pair", "ga"), None),
            P("ga", "pair"),
            P("pair"),
        ),
        out_specs=(P(("pair", "ga"), None), P(("ga", "pair"), None)),
        check_vma=False,
    )
```
